32 devices in a mesh: group: 2 (over x), ep: 16 (over z, y, core).
Axes of the slice: x: 2, y: 2, z: 4, core: 2. Of those that a mesh axis runs over, the one named last changes fastest.
Arguments:
- hidden: bfloat16 [2048, 3584], P(('group', 'ep')), parts along dimension 0, may hold values from -6 to 6
- lengths: int32 [64], P(('group', 'ep')), parts along dimension 0, may hold values from 16 to 32
- norm_gain: float32 [3584], replicated, may hold values from 0.25 to 1.75
- w_gate: bfloat16 [16, 3584, 256], P('ep'), may hold values from -0.09375 to 0.09375
- w_up: bfloat16 [16, 3584, 256], P('ep'), may hold values from -0.09375 to 0.09375
- w_down: bfloat16 [16, 256, 3584], P('ep'), may hold values from -0.1875 to 0.1875
- expert_ids: int32 [2048, 2], P(('group', 'ep')), parts along dimension 0, may hold values from 0 to 3, all different within a row; in each aligned block of 64 rows (0 to 63, 64 to 127, ...) at most 48 rows name the same one
- gate_weights: float32 [2048, 2], P(('group', 'ep')), parts along dimension 0, may hold values from 0.3 to 1.5
Outputs:
- moe_out: bfloat16 [2048, 3584], P(('group', 'ep')), parts along dimension 0
The draws below stay inside these ranges and needn't reach their ends.
There are 2 independent parts, one for each index of `group`. The reference program is written for one: setup_inputs(seed, part) draws one part's arguments, and reference() takes and returns one part's arrays. A program takes and returns all parts, laid end to end along the dimension named above; an argument that names none is the same for every part. Nothing has to cross between parts.
Inputs may be any that keep to these rules, and one draw needn't show every extreme that they name: `expert_ids`: within the 64 rows of one rank no expert is chosen more than 48 times; a token's choices differ.
All inputs are finite; a program needn't handle non-finite values.
Results may differ from the reference program's by a relative error of at most 0.0052.
Values may be sent and summed in bfloat16 or wider, within the bound.
No kernel may reach another device: no remote copies, remote signals or barrier semaphores. Data moves between devices by JAX's collectives and lax.ppermute only.
A program may use at most 128 MiB of HBM per device.

```python
import math
import jax
import jax.numpy as jnp
import numpy as np
from jax import lax

D = 3584
FF_DEV = 256
SPLIT = 4
TOPK = 2
PCAP = 32
EXPERT_FF = 1024
EXPERTS = 4
TOK_DEV = 64
TOKENS = 1024
CAP = 48
N_EP = 16


def draw_lengths(key, part):
    key = jax.random.fold_in(key, 7)
    first_key, second_key = jax.random.split(key)
    count = TOKENS // PCAP
    values = jax.random.randint(first_key, (count,), PCAP // 2, PCAP + 1)
    longest = jax.random.randint(second_key, (), 0, count)
    spots = jnp.arange(count, dtype=jnp.int32)
    return jnp.where(spots == longest, PCAP, values).astype(jnp.int32)


def levels(stream_key, dims, shards, low, top_value):
    def one(axis_at, shards_of):
        steps = jax.random.uniform(jax.random.fold_in(jax.random.fold_in(stream_key, 6), axis_at), (shards_of,), jnp.float32, low / len(shards), top_value / len(shards))
        return jnp.repeat(jnp.exp(steps), dims[axis_at] // shards_of).reshape((-1,) + (1,) * (len(dims) - axis_at - 1))

    loudness = one(*shards[0])
    for cut in shards[1:]:
        loudness = loudness * one(*cut)
    return loudness


def routed_block(rng, own, number, rows, count, top, limit, slope):
    sequence = jax.random.permutation(rng, count)
    packed, common = shares(count, rows * top, limit, slope, True), shares(count, rows * top, limit, slope, False)
    places = jnp.arange(count)

    def named(tallies, rotation):
        used = int((tallies > 0).sum())
        fixed = max(1, used // 4)
        passed = fixed + (places - fixed + rotation * (used - fixed)) % max(1, count - fixed)
        return jnp.zeros((count,), jnp.int32).at[sequence[jnp.where(places < fixed, places, passed)]].set(jnp.asarray(tallies, jnp.int32))

    tallies = jnp.where(number % 4 == 0, named(packed, number // 4), named(common, number - number // 4 - 1))
    mixed = jax.random.permutation(jax.random.fold_in(own, 3), count)
    donor, receiver = mixed[0:count // 2 * 2:2], mixed[1:count // 2 * 2:2]
    room = jnp.minimum(tallies[donor] - 1, limit - tallies[receiver]) // 2
    room = jnp.where((donor == sequence[0]) | (receiver == sequence[0]) | (tallies[receiver] == 0), 0, jnp.maximum(room, 0))
    passed = jax.random.randint(jax.random.fold_in(own, 4), (count // 2,), 0, 1 << 20) % (room + 1)
    tallies = tallies.at[donor].add(-passed).at[receiver].add(passed)
    items = jnp.searchsorted(jnp.cumsum(tallies), jnp.arange(rows * top), side="right").astype(jnp.int32)
    grid = items.reshape(top, rows).T
    grid = grid[jax.random.permutation(jax.random.fold_in(own, 1), rows)]
    rotation = jax.random.randint(jax.random.fold_in(own, 2), (rows, 1), 0, top)
    return jnp.take_along_axis(grid, (jnp.arange(top)[None, :] + rotation) % top, axis=1)


def shares(number_of, total, bound, slope, full):
    portions = [(1 << 20) // math.isqrt(standing ** slope) + 1 for standing in range(1, number_of + 1)]
    largest = bound if full else min(bound, max(-(-total // number_of), total * portions[0] // sum(portions)))
    least = 1 if total - largest >= number_of - 1 else 0
    given, surplus = [largest] + [least] * (number_of - 1), total - largest - least * (number_of - 1)
    while surplus > 0:
        movable = [i for i in range(1, number_of) if given[i] < largest] or [i for i in range(1, number_of) if given[i] < bound]
        pool, left = sum([portions[i] for i in movable]), surplus
        for i in movable:
            addition = min(bound - given[i], max(1, left * portions[i] // pool), surplus)
            given[i] = given[i] + addition
            surplus = surplus - addition
    return np.array(given)


def gaussian(own_key, dims, width, limit, pieces=(), kind=jnp.bfloat16):
    entries = jax.random.normal(own_key, dims, jnp.float32) * width
    if len(pieces) > 0:
        entries = levels(own_key, dims, pieces, -0.22, 0.18) * entries
    return jnp.clip(entries, min=-limit, max=limit).astype(kind)


def setup_inputs(seed: int = 0, part: int = 0) -> dict:
    arg_keys = jax.random.split(jax.random.key(seed), 9)
    part_keys = jax.random.split(jax.random.fold_in(arg_keys[8], part), 9)
    hidden = gaussian(part_keys[0], (TOKENS, D), 1.0, 6.0, ((0, 16),))
    lengths = draw_lengths(jax.random.fold_in(jax.random.fold_in(arg_keys[8], part), 71), part)
    norm_gain = jnp.clip(1.0 + 0.15 * jax.random.normal(arg_keys[2], (D,), jnp.float32), 0.25, 1.75)
    w_gate = gaussian(arg_keys[3], (N_EP, D, FF_DEV), D ** -0.5, 0.09375, ((0, 16),))
    w_up = gaussian(arg_keys[4], (N_EP, D, FF_DEV), D ** -0.5, 0.09375, ((0, 16),))
    w_down = gaussian(arg_keys[5], (N_EP, FF_DEV, D), EXPERT_FF ** -0.5, 0.1875, ((0, 16),))
    expert_ids_keys = jax.random.split(jax.random.fold_in(part_keys[6], 1), TOKENS // TOK_DEV)
    expert_ids_turns = jax.random.permutation(jax.random.fold_in(part_keys[6], 3), TOKENS // TOK_DEV)
    expert_ids = jax.vmap(lambda own, number: routed_block(jax.random.fold_in(part_keys[6], 2), own, number, TOK_DEV, EXPERTS, TOPK, CAP, 2))(expert_ids_keys, expert_ids_turns).reshape((TOKENS, TOPK))
    gate_weights = jnp.clip(0.3 + 1.2 * jax.random.uniform(part_keys[7], (TOKENS, TOPK), jnp.float32) ** levels(part_keys[7], (TOKENS, TOPK), ((0, 16),), -0.2, 0.2), 0.3, 1.5)
    return dict(hidden=hidden, lengths=lengths, norm_gain=norm_gain, w_gate=w_gate, w_up=w_up, w_down=w_down, expert_ids=expert_ids, gate_weights=gate_weights)


def reference(hidden, lengths, norm_gain, w_gate, w_up, w_down, expert_ids, gate_weights):
    hidden_f = hidden.astype(jnp.float32)
    meansq = lax.optimization_barrier(jnp.mean(hidden_f * hidden_f, axis=-1, keepdims=True))
    normed = (hidden_f * lax.rsqrt(meansq + 1e-06) * norm_gain).astype(jnp.bfloat16)
    position = jnp.arange(TOKENS, dtype=jnp.int32)
    prompt_of = (position // PCAP).astype(jnp.int32)
    live = position % PCAP < lengths[prompt_of]
    expert_line = jnp.arange(EXPERTS, dtype=jnp.int32)
    hits_three = (expert_ids[:, :, None] == expert_line[None, None, :]) & live[:, None, None]
    hits = lax.optimization_barrier(jnp.sum(hits_three.astype(jnp.int32), axis=1)).astype(jnp.int32)
    weight = lax.optimization_barrier(jnp.sum(jnp.where(hits_three, gate_weights[:, :, None], jnp.float32(0.0)), axis=1))
    ranked = hits.reshape(N_EP, TOK_DEV, EXPERTS)
    before = (jnp.cumsum(ranked, axis=1) - ranked).astype(jnp.int32).reshape(TOKENS, EXPERTS)
    rank_of = (position // TOK_DEV).astype(jnp.int32)
    dest = jnp.where(hits > 0, rank_of[:, None] * CAP + before, N_EP * CAP).astype(jnp.int32)
    table = jnp.full((EXPERTS, N_EP * CAP + 1), TOKENS, jnp.int32)
    sources = jnp.broadcast_to(position[:, None], (TOKENS, EXPERTS)).astype(jnp.int32)
    table = table.at[expert_line[None, :], dest].set(sources)
    table = table[:, :N_EP * CAP]
    normed_pad = jnp.concatenate([normed, jnp.zeros((1, D), jnp.bfloat16)], axis=0)
    weight_pad = jnp.concatenate([weight, jnp.zeros((1, EXPERTS), jnp.float32)], axis=0)
    gates_all = w_gate.reshape(EXPERTS, SPLIT, D, FF_DEV)
    ups_all = w_up.reshape(EXPERTS, SPLIT, D, FF_DEV)
    downs_all = w_down.reshape(EXPERTS, SPLIT, FF_DEV, D)

    def one_expert(total, item):
        index, row_ids, gate_e, up_e, down_e = item
        rows = normed_pad[row_ids]
        summed = jnp.zeros((N_EP * CAP, D), jnp.float32)
        for piece in range(SPLIT):
            gate_p = jnp.dot(rows, gate_e[piece], preferred_element_type=jnp.float32)
            up_p = jnp.dot(rows, up_e[piece], preferred_element_type=jnp.float32)
            act = (jax.nn.silu(gate_p) * up_p).astype(jnp.bfloat16)
            part = jnp.dot(act, down_e[piece], preferred_element_type=jnp.float32).astype(jnp.bfloat16)
            summed = summed + part.astype(jnp.float32)
        row_weight = weight_pad[row_ids, index]
        return (total.at[row_ids].add(row_weight[:, None] * summed), None)
    start = jnp.zeros((TOKENS + 1, D), jnp.float32)
    routed, _ = lax.scan(one_expert, start, (expert_line, table, gates_all, ups_all, downs_all))
    moe_out = (hidden_f + routed[:TOKENS]).astype(jnp.bfloat16)
    return moe_out
```

```python
import jax
import jax.numpy as jnp
from jax import lax
from jax.sharding import PartitionSpec as P

SPLIT = 4


def body(hidden, lengths, norm_gain, w_gate, w_up, w_down, expert_ids, gate_weights):
    tokens_here, width = hidden.shape
    prompts = lengths.shape[0]
    slots_per = tokens_here // prompts
    topk = expert_ids.shape[1]
    ranks = lax.axis_size("ep")
    experts = ranks // SPLIT
    capacity = SPLIT * ((3 * tokens_here * topk + 2 * experts * SPLIT - 1) // (2 * experts * SPLIT))
    plane = lax.axis_index("ep") // SPLIT

    swap_core = [(i, i ^ 1) for i in range(ranks)]
    swap_side = [(i, i ^ 2) for i in range(ranks)]

    def shift(d):
        return [(i, (i + SPLIT * d) % ranks) for i in range(ranks)]

    gates = (w_gate[0], lax.ppermute(w_gate[0], "ep", swap_core))
    ups = (w_up[0], lax.ppermute(w_up[0], "ep", swap_core))
    downs = (w_down[0], lax.ppermute(w_down[0], "ep", swap_core))

    position = jnp.arange(tokens_here, dtype=jnp.int32)
    prompt_line = jnp.arange(prompts, dtype=jnp.int32)
    inside = (position // slots_per)[:, None] == prompt_line[None, :]
    below = (position % slots_per)[:, None] < lengths[None, :]
    live = jnp.any(inside & below, axis=1)
    hidden_f = hidden.astype(jnp.float32)
    meansq = jnp.mean(hidden_f * hidden_f, axis=-1, keepdims=True)
    normed = (hidden_f * lax.rsqrt(meansq + 1e-06) * norm_gain).astype(jnp.bfloat16)

    away = (expert_ids - plane + experts) % experts
    distance_line = jnp.arange(experts, dtype=jnp.int32)
    onehot = ((away[:, :, None] == distance_line) & live[:, None, None]).astype(jnp.float32)
    chosen = jnp.sum(onehot, axis=1)
    weight = jnp.sum(onehot * gate_weights[:, :, None], axis=1)
    before = jnp.cumsum(chosen, axis=0) - chosen
    slot_line = jnp.arange(capacity, dtype=jnp.float32)
    placed = ((before[:, :, None] == slot_line) & (chosen[:, :, None] > 0)).astype(jnp.bfloat16)
    picker = placed.reshape(tokens_here, experts * capacity).T
    packed = jnp.dot(picker, normed, preferred_element_type=jnp.float32).astype(jnp.bfloat16)
    packed = packed.reshape(experts, capacity, width)

    def expert(rows):
        total = None
        for gate, up, down in zip(gates, ups, downs):
            gate_p = jnp.dot(rows, gate, preferred_element_type=jnp.float32)
            up_p = jnp.dot(rows, up, preferred_element_type=jnp.float32)
            act = (jax.nn.silu(gate_p) * up_p).astype(jnp.bfloat16)
            part = jnp.dot(act, down, preferred_element_type=jnp.float32)
            total = part if total is None else total + part
        return total

    if experts == 4:
        groups = [[0], [2], [1, 3]]
    else:
        groups = [[d] for d in range(experts)]

    arrived = {0: packed[0]}
    for d in [d for g in groups for d in g if d]:
        arrived[d] = lax.ppermute(packed[d], "ep", shift(d))

    routed = jnp.zeros((tokens_here, width), jnp.float32)
    for g in groups:
        mine = jnp.concatenate([arrived[d] for d in g]) if len(g) > 1 else arrived[g[0]]
        theirs = lax.ppermute(mine, "ep", swap_side)
        part = expert(jnp.concatenate([mine, theirs]))
        half = mine.shape[0]
        other = lax.ppermute(part[half:].astype(jnp.bfloat16), "ep", swap_side)
        summed = (part[:half] + other.astype(jnp.float32)).astype(jnp.bfloat16)
        for k, d in enumerate(g):
            rows = summed[k * capacity : (k + 1) * capacity]
            if d:
                rows = lax.ppermute(rows, "ep", shift(experts - d))
            taken = jnp.dot(placed[:, d], rows, preferred_element_type=jnp.float32)
            routed = routed + weight[:, d : d + 1] * taken
    return (hidden_f + routed).astype(jnp.bfloat16)


def solution(mesh):
    return jax.shard_map(
        body,
        mesh=mesh,
        in_specs=(
            P(("group", "ep"), None),
            P(("group", "ep")),
            P(),
            P("ep", None, None),
            P("ep", None, None),
            P("ep", None, None),
            P(("group", "ep"), None),
            P(("group", "ep"), None),
        ),
        out_specs=P(("group", "ep"), None),
        check_vma=False,
    )
```

```python
import functools

import jax
import jax.numpy as jnp
from jax import lax
from jax.experimental import pallas as pl
from jax.experimental.pallas import tpu as pltpu
from jax.sharding import PartitionSpec as P

SPLIT = 4
LANES = 128
VMEM = pl.BlockSpec(memory_space=pltpu.VMEM)
SMEM = pl.BlockSpec(memory_space=pltpu.SMEM)
ANY = pl.BlockSpec(memory_space=pl.ANY)


def dot(a, b):
    return jnp.dot(a, b, preferred_element_type=jnp.float32)


def columns_of(width):
    return next(c for c in (512, 256, 128, width) if width % c == 0)


def pack_kernel(experts, capacity, plane_ref, lengths_ref, hidden_ref, gain_ref, ids_ref, gates_ref, *outs):
    packed_refs, slot_ref, weight_ref = outs[:experts], outs[experts], outs[experts + 1]
    tokens, width = hidden_ref.shape
    prompts = lengths_ref.shape[0]
    slots_per = tokens // prompts
    row = lax.broadcasted_iota(jnp.int32, (tokens, 1), 0)
    live = row < 0
    for p in range(prompts):
        live = live | ((row >= p * slots_per) & (row < p * slots_per + lengths_ref[p]))
    lane = lax.broadcasted_iota(jnp.int32, (tokens, LANES), 1)
    chosen = jnp.zeros((tokens, LANES), jnp.float32)
    weight = jnp.zeros((tokens, LANES), jnp.float32)
    for k in range(ids_ref.shape[1]):
        away = ids_ref[:, k : k + 1] - plane_ref[0]
        away = jnp.where(away < 0, away + experts, away)
        hit = ((away == lane) & live).astype(jnp.float32)
        chosen += hit
        weight += hit * gates_ref[:, k : k + 1]
    below = lax.broadcasted_iota(jnp.int32, (tokens, tokens), 1) < lax.broadcasted_iota(
        jnp.int32, (tokens, tokens), 0
    )
    before = dot(below.astype(jnp.bfloat16), chosen.astype(jnp.bfloat16))
    slot = jnp.where(chosen > 0, before, -1.0)
    slot_ref[...] = slot
    weight_ref[...] = weight
    slot_t = slot.T

    hidden = hidden_ref[...].astype(jnp.float32)
    meansq = jnp.mean(hidden * hidden, axis=-1, keepdims=True)
    scale = lax.rsqrt(meansq + 1e-06)
    line = lax.broadcasted_iota(jnp.int32, (capacity, tokens), 0).astype(jnp.float32)
    picker = jnp.concatenate(
        [(line == slot_t[d : d + 1, :]).astype(jnp.float32) for d in range(experts)]
    ).astype(jnp.bfloat16)
    step = columns_of(width)
    for c in range(0, width, step):
        normed = hidden_ref[:, c : c + step].astype(jnp.float32) * scale * gain_ref[:, c : c + step]
        rows = dot(picker, normed.astype(jnp.bfloat16)).astype(jnp.bfloat16)
        for d in range(experts):
            packed_refs[d][:, c : c + step] = rows[d * capacity : (d + 1) * capacity]


def expert_kernel(mine_ref, theirs_ref, *refs):
    weights, (own_ref, sent_ref), held, sems = refs[:6], refs[6:8], refs[8:14], refs[14]
    copies = [pltpu.make_async_copy(weights[i], held[i], sems.at[i]) for i in range(6)]
    for copy in copies:
        copy.start()
    half, width = mine_ref.shape
    rows = jnp.concatenate([mine_ref[...], theirs_ref[...]])
    acts = []
    for k in range(2):
        copies[3 * k].wait()
        gate_p = dot(rows, held[3 * k][...])
        copies[3 * k + 1].wait()
        up_p = dot(rows, held[3 * k + 1][...])
        acts.append((jax.nn.silu(gate_p) * up_p).astype(jnp.bfloat16))
    copies[2].wait()
    copies[5].wait()
    step = columns_of(width)
    for c in range(0, width, step):
        part = dot(acts[0], held[2][:, c : c + step]) + dot(acts[1], held[5][:, c : c + step])
        own_ref[:, c : c + step] = part[:half]
        sent_ref[:, c : c + step] = part[half:].astype(jnp.bfloat16)


def mix_kernel(experts, capacity, hidden_ref, slot_ref, weight_ref, own_ref, other_ref, *refs):
    rows_refs, out_ref = refs[:-1], refs[-1]
    tokens, width = hidden_ref.shape
    line = lax.broadcasted_iota(jnp.int32, (tokens, capacity), 1).astype(jnp.float32)
    placed = [(line == slot_ref[:, d : d + 1]).astype(jnp.bfloat16) for d in range(experts)]
    step = columns_of(width)
    for c in range(0, width, step):
        cols = slice(c, c + step)
        total = hidden_ref[:, cols].astype(jnp.float32)
        for d in range(experts):
            if d:
                rows = rows_refs[d - 1][:, cols]
            else:
                rows = (own_ref[:, cols] + other_ref[:, cols].astype(jnp.float32)).astype(jnp.bfloat16)
            total += weight_ref[:, d : d + 1] * dot(placed[d], rows)
        out_ref[:, cols] = total.astype(jnp.bfloat16)


def body(hidden, lengths, norm_gain, w_gate, w_up, w_down, expert_ids, gate_weights):
    tokens_here, width = hidden.shape
    topk = expert_ids.shape[1]
    ranks = lax.axis_size("ep")
    experts = ranks // SPLIT
    capacity = SPLIT * ((3 * tokens_here * topk + 2 * experts * SPLIT - 1) // (2 * experts * SPLIT))
    capacity = -(-capacity // 16) * 16
    ff = w_gate.shape[-1]
    plane = (lax.axis_index("ep") // SPLIT).astype(jnp.int32).reshape(1)

    swap_core = [(i, i ^ 1) for i in range(ranks)]
    swap_side = [(i, i ^ 2) for i in range(ranks)]

    def shift(d):
        return [(i, (i + SPLIT * d) % ranks) for i in range(ranks)]

    def struct(rows, cols, dtype):
        return jax.ShapeDtypeStruct((rows, cols), dtype)

    block = struct(capacity, width, jnp.bfloat16)
    *packed, slot, weight = pl.pallas_call(
        functools.partial(pack_kernel, experts, capacity),
        out_shape=[block] * experts + [struct(tokens_here, LANES, jnp.float32)] * 2,
        in_specs=[SMEM, SMEM, VMEM, VMEM, VMEM, VMEM],
        out_specs=[VMEM] * (experts + 2),
        compiler_params=pltpu.CompilerParams(vmem_limit_bytes=16 << 20),
    )(plane, lengths, hidden, norm_gain.reshape(1, width), expert_ids, gate_weights)

    own_weights = (w_gate[0], w_up[0], w_down[0])
    weights = own_weights + tuple(lax.ppermute(w, "ep", swap_core) for w in own_weights)

    flops = 2 * 2 * capacity * width * ff * 6
    expert = pl.pallas_call(
        expert_kernel,
        out_shape=[struct(capacity, width, jnp.float32), block],
        in_specs=[VMEM, VMEM] + [ANY] * 6,
        out_specs=[VMEM, VMEM],
        scratch_shapes=[pltpu.VMEM(w.shape, w.dtype) for w in weights] + [pltpu.SemaphoreType.DMA((6,))],
        compiler_params=pltpu.CompilerParams(vmem_limit_bytes=28 << 20),
        cost_estimate=pl.CostEstimate(
            flops=flops, bytes_accessed=12 * width * ff, transcendentals=4 * capacity * ff
        ),
    )

    if experts == 4:
        order = [0, 2, 1, 3]
    else:
        order = list(range(experts))
    arrived = {d: lax.ppermute(packed[d], "ep", shift(d)) if d else packed[0] for d in order}
    back = {}
    for d in order:
        own, sent = expert(arrived[d], lax.ppermute(arrived[d], "ep", swap_side), *weights)
        other = lax.ppermute(sent, "ep", swap_side)
        if d:
            rows = (own + other.astype(jnp.float32)).astype(jnp.bfloat16)
            back[d] = lax.ppermute(rows, "ep", shift(experts - d))
        else:
            back[0] = (own, other)
    return pl.pallas_call(
        functools.partial(mix_kernel, experts, capacity),
        out_shape=struct(tokens_here, width, jnp.bfloat16),
        in_specs=[VMEM] * (experts + 4),
        out_specs=VMEM,
        compiler_params=pltpu.CompilerParams(vmem_limit_bytes=16 << 20),
    )(hidden, slot, weight, *back[0], *(back[d] for d in range(1, experts)))


def solution(mesh):
    return jax.shard_map(
        body,
        mesh=mesh,
        in_specs=(
            P(("group", "ep"), None),
            P(("group", "ep")),
            P(),
            P("ep", None, None),
            P("ep", None, None),
            P("ep", None, None),
            P(("group", "ep"), None),
            P(("group", "ep"), None),
        ),
        out_specs=P(("group", "ep"), None),
        check_vma=False,
    )
```

```python
import functools

import jax
import jax.numpy as jnp
from jax import lax
from jax.experimental import pallas as pl
from jax.experimental.pallas import tpu as pltpu
from jax.sharding import PartitionSpec as P

SPLIT = 4
VMEM_BYTES = 60 << 20
VMEM = pl.BlockSpec(memory_space=pltpu.VMEM)
SMEM = pl.BlockSpec(memory_space=pltpu.SMEM)
HBM = pl.BlockSpec(memory_space=pltpu.HBM)


def dot(a, b):
    return jnp.dot(a, b, preferred_element_type=jnp.float32)


def columns_of(width):
    return next(c for c in (512, 256, 128, width) if width % c == 0)


def pack_kernel(experts, capacity, plane_ref, lengths_ref, hidden_ref, gain_ref, ids_ref, gates_ref, *outs):
    packed_refs, slot_ref, weight_ref = outs[:experts], outs[experts], outs[experts + 1]
    tokens, width = hidden_ref.shape
    prompts = lengths_ref.shape[0]
    slots_per = tokens // prompts
    column = lax.broadcasted_iota(jnp.int32, (1, tokens), 1)
    live = column < 0
    for p in range(prompts):
        live = live | ((column >= p * slots_per) & (column < p * slots_per + lengths_ref[p]))
    lines = slot_ref.shape[1]
    line = lax.broadcasted_iota(jnp.int32, (lines, tokens), 0)
    chosen = jnp.zeros((lines, tokens), jnp.float32)
    weight = jnp.zeros((lines, tokens), jnp.float32)
    for k in range(ids_ref.shape[0]):
        away = ids_ref[k : k + 1, :] - plane_ref[0]
        away = jnp.where(away < 0, away + experts, away)
        hit = ((away == line) & live).astype(jnp.float32)
        chosen += hit
        weight += hit * gates_ref[k : k + 1, :]
    earlier = lax.broadcasted_iota(jnp.int32, (tokens, tokens), 0) < lax.broadcasted_iota(
        jnp.int32, (tokens, tokens), 1
    )
    before = dot(chosen.astype(jnp.bfloat16), earlier.astype(jnp.bfloat16))
    slot = jnp.where(chosen > 0, before, -1.0)
    slot_ref[...] = slot.T
    weight_ref[...] = weight.T

    hidden = hidden_ref[...].astype(jnp.float32)
    meansq = jnp.mean(hidden * hidden, axis=-1, keepdims=True)
    scale = lax.rsqrt(meansq + 1e-06)
    place = lax.broadcasted_iota(jnp.int32, (capacity, tokens), 0).astype(jnp.float32)
    picker = jnp.concatenate(
        [(place == slot[d : d + 1, :]).astype(jnp.float32) for d in range(experts)]
    ).astype(jnp.bfloat16)
    step = columns_of(width)
    for c in range(0, width, step):
        normed = hidden_ref[:, c : c + step].astype(jnp.float32) * scale * gain_ref[c : c + step][None, :]
        rows = dot(picker, normed.astype(jnp.bfloat16)).astype(jnp.bfloat16)
        for d in range(experts):
            packed_refs[d][:, c : c + step] = rows[d * capacity : (d + 1) * capacity]


def activate(rows, gate_ref, up_ref):
    return (jax.nn.silu(dot(rows, gate_ref[...])) * dot(rows, up_ref[...])).astype(jnp.bfloat16)


def first_kernel(rows_ref, gate_ref, up_ref, down_ref, out_ref):
    act = activate(rows_ref[...], gate_ref, up_ref)
    step = columns_of(out_ref.shape[1])
    for c in range(0, out_ref.shape[1], step):
        out_ref[:, c : c + step] = dot(act, down_ref[:, c : c + step])


def expert_kernel(begun, mine_ref, theirs_ref, *refs):
    weights, (own_ref, sent_ref) = refs[:6], refs[-2:]
    half, width = mine_ref.shape
    rows = jnp.concatenate([mine_ref[...], theirs_ref[...]])
    near = activate(theirs_ref[...] if begun else rows, *weights[:2])
    far = activate(rows, *weights[3:5])
    step = columns_of(width)
    for c in range(0, width, step):
        cols = slice(c, c + step)
        part, other = dot(near, weights[2][:, cols]), dot(far, weights[5][:, cols])
        here = refs[6][:, cols] if begun else part[:half]
        own_ref[:, cols] = here + other[:half]
        sent_ref[:, cols] = (part[-half:] + other[half:]).astype(jnp.bfloat16)


def mix_kernel(experts, capacity, hidden_ref, slot_ref, weight_ref, own_ref, other_ref, *refs):
    rows_refs, out_ref = refs[:-1], refs[-1]
    tokens, width = hidden_ref.shape
    line = lax.broadcasted_iota(jnp.int32, (tokens, capacity), 1).astype(jnp.float32)
    placed = [(line == slot_ref[:, d : d + 1]).astype(jnp.bfloat16) for d in range(experts)]
    step = columns_of(width)
    for c in range(0, width, step):
        cols = slice(c, c + step)
        total = hidden_ref[:, cols].astype(jnp.float32)
        for d in range(experts):
            if d:
                rows = rows_refs[d - 1][:, cols]
            else:
                rows = (own_ref[:, cols] + other_ref[:, cols].astype(jnp.float32)).astype(jnp.bfloat16)
            total += weight_ref[:, d : d + 1] * dot(placed[d], rows)
        out_ref[:, cols] = total.astype(jnp.bfloat16)


def body(hidden, lengths, norm_gain, w_gate, w_up, w_down, expert_ids, gate_weights):
    tokens_here, width = hidden.shape
    topk = expert_ids.shape[1]
    ranks = lax.axis_size("ep")
    experts = ranks // SPLIT
    capacity = SPLIT * ((3 * tokens_here * topk + 2 * experts * SPLIT - 1) // (2 * experts * SPLIT))
    capacity = -(-capacity // 16) * 16
    ff = w_gate.shape[-1]
    plane = (lax.axis_index("ep") // SPLIT).astype(jnp.int32).reshape(1)

    swap_core = [(i, i ^ 1) for i in range(ranks)]
    swap_side = [(i, i ^ 2) for i in range(ranks)]

    def shift(d):
        return [(i, (i + SPLIT * d) % ranks) for i in range(ranks)]

    def struct(rows, cols, dtype):
        return jax.ShapeDtypeStruct((rows, cols), dtype)

    lines = max(8, -(-experts // 8) * 8)
    block = struct(capacity, width, jnp.bfloat16)
    *packed, slot, weight = pl.pallas_call(
        functools.partial(pack_kernel, experts, capacity),
        out_shape=[block] * experts + [struct(tokens_here, lines, jnp.float32)] * 2,
        in_specs=[SMEM, SMEM, VMEM, VMEM, VMEM, VMEM],
        out_specs=[VMEM] * (experts + 2),
        compiler_params=pltpu.CompilerParams(vmem_limit_bytes=VMEM_BYTES),
    )(plane, lengths, hidden, norm_gain, expert_ids.T, gate_weights.T)

    def after(value, *others):
        return lax.optimization_barrier((value, *others))[0]

    params = dict(
        compiler_params=pltpu.CompilerParams(vmem_limit_bytes=32 << 20),
        cost_estimate=pl.CostEstimate(flops=1, bytes_accessed=1, transcendentals=0),
    )

    def expert(*operands):
        return pl.pallas_call(
            functools.partial(expert_kernel, len(operands) > 8),
            out_shape=[struct(capacity, width, jnp.float32), block],
            in_specs=[VMEM] * len(operands),
            out_specs=[VMEM, VMEM],
            **params,
        )(*operands)

    def first(*operands):
        return pl.pallas_call(
            first_kernel,
            out_shape=struct(capacity, width, jnp.float32),
            in_specs=[VMEM] * 4,
            out_specs=VMEM,
            **params,
        )(*operands)

    def across(rows):
        return lax.ppermute(rows, "ep", swap_side)

    order = [2, 1, 3] if experts == 4 else list(range(1, experts))
    count = len(order)
    theirs = across(packed[0])
    arrived = [lax.ppermute(packed[order[0]], "ep", shift(order[0]))]
    own_weights = (w_gate[0], w_up[0], w_down[0])
    weights = own_weights + tuple(lax.ppermute(after(w, packed[0]), "ep", swap_core) for w in own_weights)

    def send_along(i, *tied):
        arrived.append(lax.ppermute(after(packed[order[i]], *tied), "ep", shift(order[i])))

    own_here, sent_here = expert(packed[0], theirs, *weights, first(packed[0], *own_weights))
    other_here = across(sent_here)
    crossed = [across(after(arrived[0], sent_here))]
    if count > 1:
        send_along(1, arrived[0], sent_here)
    own, sent, other, rows, back = [], [], [], [], {}

    def send_back(i, *tied):
        rows.append((own[i] + after(other[i], *tied).astype(jnp.float32)).astype(jnp.bfloat16))
        back[order[i]] = lax.ppermute(rows[i], "ep", shift(experts - order[i]))

    for i in range(count):
        tied = [] if i else [other_here]
        if i > 1:
            tied.append(rows[i - 2])
        if i + 1 < count:
            crossed.append(across(after(arrived[i + 1], sent[i - 1] if i else other_here)))
            tied.append(arrived[i + 1])
        if i + 2 < count:
            send_along(i + 2, arrived[i + 1])
        mine_sum, their_part = expert(arrived[i], after(crossed[i], *tied), *weights)
        own.append(mine_sum)
        sent.append(their_part)
        if i:
            send_back(i - 1, sent[i])
        other.append(across(after(sent[i], rows[i - 1]) if i else sent[i]))
    send_back(count - 1, *(back[d] for d in order[:-2]))
    back[0] = (own_here, other_here)
    return pl.pallas_call(
        functools.partial(mix_kernel, experts, capacity),
        out_shape=struct(tokens_here, width, jnp.bfloat16),
        in_specs=[VMEM] * (experts + 4),
        out_specs=VMEM,
        compiler_params=pltpu.CompilerParams(vmem_limit_bytes=16 << 20),
    )(hidden, slot, weight, *back[0], *(back[d] for d in range(1, experts)))


def solution(mesh):
    return jax.shard_map(
        body,
        mesh=mesh,
        in_specs=(
            P(("group", "ep"), None),
            P(("group", "ep")),
            P(),
            P("ep", None, None),
            P("ep", None, None),
            P("ep", None, None),
            P(("group", "ep"), None),
            P(("group", "ep"), None),
        ),
        out_specs=P(("group", "ep"), None),
        check_vma=False,
    )
```

```python
import functools

import jax
import jax.numpy as jnp
from jax import lax
from jax.experimental import pallas as pl
from jax.experimental.pallas import tpu as pltpu
from jax.sharding import PartitionSpec as P

SPLIT = 4
VMEM_BYTES = 60 << 20
VMEM = pl.BlockSpec(memory_space=pltpu.VMEM)
SMEM = pl.BlockSpec(memory_space=pltpu.SMEM)
HBM = pl.BlockSpec(memory_space=pltpu.HBM)


def dot(a, b):
    return jnp.dot(a, b, preferred_element_type=jnp.float32)


def columns_of(width):
    return next(c for c in (512, 256, 128, width) if width % c == 0)


def pack_kernel(experts, capacity, plane_ref, lengths_ref, hidden_ref, gain_ref, ids_ref, gates_ref, *outs):
    packed_refs, slot_ref, weight_ref = outs[:experts], outs[experts], outs[experts + 1]
    tokens, width = hidden_ref.shape
    prompts = lengths_ref.shape[0]
    slots_per = tokens // prompts
    column = lax.broadcasted_iota(jnp.int32, (1, tokens), 1)
    live = column < 0
    for p in range(prompts):
        live = live | ((column >= p * slots_per) & (column < p * slots_per + lengths_ref[p]))
    lines = slot_ref.shape[1]
    line = lax.broadcasted_iota(jnp.int32, (lines, tokens), 0)
    chosen = jnp.zeros((lines, tokens), jnp.float32)
    weight = jnp.zeros((lines, tokens), jnp.float32)
    for k in range(ids_ref.shape[0]):
        away = ids_ref[k : k + 1, :] - plane_ref[0]
        away = jnp.where(away < 0, away + experts, away)
        hit = ((away == line) & live).astype(jnp.float32)
        chosen += hit
        weight += hit * gates_ref[k : k + 1, :]
    earlier = lax.broadcasted_iota(jnp.int32, (tokens, tokens), 0) < lax.broadcasted_iota(
        jnp.int32, (tokens, tokens), 1
    )
    before = dot(chosen.astype(jnp.bfloat16), earlier.astype(jnp.bfloat16))
    slot = jnp.where(chosen > 0, before, -1.0)
    slot_ref[...] = slot.T
    weight_ref[...] = weight.T

    hidden = hidden_ref[...].astype(jnp.float32)
    meansq = jnp.mean(hidden * hidden, axis=-1, keepdims=True)
    scale = lax.rsqrt(meansq + 1e-06)
    place = lax.broadcasted_iota(jnp.int32, (capacity, tokens), 0).astype(jnp.float32)
    picker = jnp.concatenate(
        [(place == slot[d : d + 1, :]).astype(jnp.float32) for d in range(experts)]
    ).astype(jnp.bfloat16)
    step = columns_of(width)
    for c in range(0, width, step):
        normed = hidden_ref[:, c : c + step].astype(jnp.float32) * scale * gain_ref[c : c + step][None, :]
        rows = dot(picker, normed.astype(jnp.bfloat16)).astype(jnp.bfloat16)
        for d in range(experts):
            packed_refs[d][:, c : c + step] = rows[d * capacity : (d + 1) * capacity]


def activate(rows, gate_ref, up_ref):
    return (jax.nn.silu(dot(rows, gate_ref[...])) * dot(rows, up_ref[...])).astype(jnp.bfloat16)


def first_kernel(rows_ref, gate_ref, up_ref, down_ref, out_ref):
    act = activate(rows_ref[...], gate_ref, up_ref)
    step = columns_of(out_ref.shape[1])
    for c in range(0, out_ref.shape[1], step):
        out_ref[:, c : c + step] = dot(act, down_ref[:, c : c + step])


def expert_kernel(begun, mine_ref, theirs_ref, *refs):
    weights, (own_ref, sent_ref) = refs[:6], refs[-2:]
    half, width = mine_ref.shape
    rows = jnp.concatenate([mine_ref[...], theirs_ref[...]])
    near = activate(theirs_ref[...] if begun else rows, *weights[:2])
    far = activate(rows, *weights[3:5])
    step = columns_of(width)
    for c in range(0, width, step):
        cols = slice(c, c + step)
        part, other = dot(near, weights[2][:, cols]), dot(far, weights[5][:, cols])
        here = refs[6][:, cols] if begun else part[:half]
        own_ref[:, cols] = here + other[:half]
        sent_ref[:, cols] = (part[-half:] + other[half:]).astype(jnp.bfloat16)


def mix_kernel(experts, capacity, hidden_ref, slot_ref, weight_ref, own_ref, other_ref, *refs):
    rows_refs, out_ref = refs[:-1], refs[-1]
    tokens, width = hidden_ref.shape
    line = lax.broadcasted_iota(jnp.int32, (tokens, capacity), 1).astype(jnp.float32)
    placed = [(line == slot_ref[:, d : d + 1]).astype(jnp.bfloat16) for d in range(experts)]
    step = columns_of(width)
    for c in range(0, width, step):
        cols = slice(c, c + step)
        total = hidden_ref[:, cols].astype(jnp.float32)
        for d in range(experts):
            if d:
                rows = rows_refs[d - 1][:, cols]
            else:
                rows = (own_ref[:, cols] + other_ref[:, cols].astype(jnp.float32)).astype(jnp.bfloat16)
            total += weight_ref[:, d : d + 1] * dot(placed[d], rows)
        out_ref[:, cols] = total.astype(jnp.bfloat16)


def body(hidden, lengths, norm_gain, w_gate, w_up, w_down, expert_ids, gate_weights):
    tokens_here, width = hidden.shape
    topk = expert_ids.shape[1]
    ranks = lax.axis_size("ep")
    experts = ranks // SPLIT
    capacity = SPLIT * ((3 * tokens_here * topk + 2 * experts * SPLIT - 1) // (2 * experts * SPLIT))
    capacity = -(-capacity // 16) * 16
    ff = w_gate.shape[-1]
    plane = (lax.axis_index("ep") // SPLIT).astype(jnp.int32).reshape(1)

    swap_core = [(i, i ^ 1) for i in range(ranks)]
    swap_side = [(i, i ^ 2) for i in range(ranks)]

    def shift(d):
        return [(i, (i + SPLIT * d) % ranks) for i in range(ranks)]

    def struct(rows, cols, dtype):
        return jax.ShapeDtypeStruct((rows, cols), dtype)

    lines = max(8, -(-experts // 8) * 8)
    block = struct(capacity, width, jnp.bfloat16)
    *packed, slot, weight = pl.pallas_call(
        functools.partial(pack_kernel, experts, capacity),
        out_shape=[block] * experts + [struct(tokens_here, lines, jnp.float32)] * 2,
        in_specs=[SMEM, SMEM, VMEM, VMEM, VMEM, VMEM],
        out_specs=[VMEM] * (experts + 2),
        compiler_params=pltpu.CompilerParams(vmem_limit_bytes=VMEM_BYTES),
    )(plane, lengths, hidden, norm_gain, expert_ids.T, gate_weights.T)

    def after(value, *others):
        return lax.optimization_barrier((value, *others))[0]

    params = dict(
        compiler_params=pltpu.CompilerParams(vmem_limit_bytes=32 << 20),
        cost_estimate=pl.CostEstimate(flops=1, bytes_accessed=1, transcendentals=0),
    )

    def expert(*operands):
        return pl.pallas_call(
            functools.partial(expert_kernel, len(operands) > 8),
            out_shape=[struct(capacity, width, jnp.float32), block],
            in_specs=[VMEM] * len(operands),
            out_specs=[VMEM, VMEM],
            **params,
        )(*operands)

    def first(*operands):
        return pl.pallas_call(
            first_kernel,
            out_shape=struct(capacity, width, jnp.float32),
            in_specs=[VMEM] * 4,
            out_specs=VMEM,
            **params,
        )(*operands)

    def across(rows):
        return lax.ppermute(rows, "ep", swap_side)

    order = [2, 1, 3] if experts == 4 else list(range(1, experts))
    count = len(order)
    theirs = across(packed[0])
    arrived = [lax.ppermute(packed[order[0]], "ep", shift(order[0]))]
    own_weights = (w_gate[0], w_up[0], w_down[0])
    weights = own_weights + tuple(lax.ppermute(after(w, packed[0]), "ep", swap_core) for w in own_weights)

    def send_along(i, *tied):
        arrived.append(lax.ppermute(after(packed[order[i]], *tied), "ep", shift(order[i])))

    own_here, sent_here = expert(packed[0], theirs, *weights, first(packed[0], *own_weights))
    other_here = across(sent_here)
    crossed = [across(after(arrived[0], other_here))]
    if count > 1:
        send_along(1, arrived[0], other_here)
    own, sent, other, rows, back = [], [], [], [], {}

    def send_back(i, *tied):
        rows.append((own[i] + after(other[i], *tied).astype(jnp.float32)).astype(jnp.bfloat16))
        back[order[i]] = lax.ppermute(rows[i], "ep", shift(experts - order[i]))

    for i in range(count):
        tied = [] if i else [other_here]
        if i > 1:
            tied.append(rows[i - 2])
        if i + 1 < count:
            crossed.append(across(after(arrived[i + 1], sent[i - 1] if i else other_here)))
            tied.append(arrived[i + 1])
        if i + 2 < count:
            send_along(i + 2, arrived[i + 1])
        mine_sum, their_part = expert(arrived[i], after(crossed[i], *tied), *weights)
        own.append(mine_sum)
        sent.append(their_part)
        if i:
            send_back(i - 1, sent[i])
        other.append(across(after(sent[i], rows[i - 1]) if i > 1 else sent[i]))
    send_back(count - 1, *(back[d] for d in order[:-2]))
    back[0] = (own_here, other_here)
    return pl.pallas_call(
        functools.partial(mix_kernel, experts, capacity),
        out_shape=struct(tokens_here, width, jnp.bfloat16),
        in_specs=[VMEM] * (experts + 4),
        out_specs=VMEM,
        compiler_params=pltpu.CompilerParams(vmem_limit_bytes=16 << 20),
    )(hidden, slot, weight, *back[0], *(back[d] for d in range(1, experts)))


def solution(mesh):
    return jax.shard_map(
        body,
        mesh=mesh,
        in_specs=(
            P(("group", "ep"), None),
            P(("group", "ep")),
            P(),
            P("ep", None, None),
            P("ep", None, None),
            P("ep", None, None),
            P(("group", "ep"), None),
            P(("group", "ep"), None),
        ),
        out_specs=P(("group", "ep"), None),
        check_vma=False,
    )
```

```python
import functools

import jax
import jax.numpy as jnp
from jax import lax
from jax.experimental import pallas as pl
from jax.experimental.pallas import tpu as pltpu
from jax.sharding import PartitionSpec as P

SPLIT = 4
VMEM_BYTES = 60 << 20
VMEM = pl.BlockSpec(memory_space=pltpu.VMEM)
SMEM = pl.BlockSpec(memory_space=pltpu.SMEM)
HBM = pl.BlockSpec(memory_space=pltpu.HBM)


def dot(a, b):
    return jnp.dot(a, b, preferred_element_type=jnp.float32)


def columns_of(width):
    return next(c for c in (1792, 512, 256, 128, width) if width % c == 0)


def pack_kernel(experts, capacity, plane_ref, lengths_ref, hidden_ref, gain_ref, ids_ref, gates_ref, *outs):
    packed_refs, slot_ref, weight_ref = outs[:experts], outs[experts], outs[experts + 1]
    tokens, width = hidden_ref.shape
    prompts = lengths_ref.shape[0]
    slots_per = tokens // prompts
    column = lax.broadcasted_iota(jnp.int32, (1, tokens), 1)
    live = column < 0
    for p in range(prompts):
        live = live | ((column >= p * slots_per) & (column < p * slots_per + lengths_ref[p]))
    lines = slot_ref.shape[1]
    line = lax.broadcasted_iota(jnp.int32, (lines, tokens), 0)
    chosen = jnp.zeros((lines, tokens), jnp.float32)
    weight = jnp.zeros((lines, tokens), jnp.float32)
    for k in range(ids_ref.shape[0]):
        away = ids_ref[k : k + 1, :] - plane_ref[0]
        away = jnp.where(away < 0, away + experts, away)
        hit = ((away == line) & live).astype(jnp.float32)
        chosen += hit
        weight += hit * gates_ref[k : k + 1, :]
    earlier = lax.broadcasted_iota(jnp.int32, (tokens, tokens), 0) < lax.broadcasted_iota(
        jnp.int32, (tokens, tokens), 1
    )
    before = dot(chosen.astype(jnp.bfloat16), earlier.astype(jnp.bfloat16))
    slot = jnp.where(chosen > 0, before, -1.0)
    slot_ref[...] = slot.T
    weight_ref[...] = weight.T

    hidden = hidden_ref[...].astype(jnp.float32)
    meansq = jnp.mean(hidden * hidden, axis=-1, keepdims=True)
    scale = lax.rsqrt(meansq + 1e-06)
    place = lax.broadcasted_iota(jnp.int32, (capacity, tokens), 0).astype(jnp.float32)
    picker = jnp.concatenate(
        [(place == slot[d : d + 1, :]).astype(jnp.float32) for d in range(experts)]
    ).astype(jnp.bfloat16)
    step = columns_of(width)
    for c in range(0, width, step):
        normed = hidden_ref[:, c : c + step].astype(jnp.float32) * scale * gain_ref[c : c + step][None, :]
        rows = dot(picker, normed.astype(jnp.bfloat16)).astype(jnp.bfloat16)
        for d in range(experts):
            packed_refs[d][:, c : c + step] = rows[d * capacity : (d + 1) * capacity]


def activate(rows, gate_ref, up_ref):
    return (jax.nn.silu(dot(rows, gate_ref[...])) * dot(rows, up_ref[...])).astype(jnp.bfloat16)


def first_kernel(rows_ref, gate_ref, up_ref, down_ref, out_ref):
    act = activate(rows_ref[...], gate_ref, up_ref)
    step = columns_of(out_ref.shape[1])
    for c in range(0, out_ref.shape[1], step):
        out_ref[:, c : c + step] = dot(act, down_ref[:, c : c + step])


def expert_kernel(begun, mine_ref, theirs_ref, *refs):
    weights, (own_ref, sent_ref) = refs[:6], refs[-2:]
    half, width = mine_ref.shape
    rows = jnp.concatenate([mine_ref[...], theirs_ref[...]])
    near = activate(theirs_ref[...] if begun else rows, *weights[:2])
    far = activate(rows, *weights[3:5])
    step = columns_of(width)
    for c in range(0, width, step):
        cols = slice(c, c + step)
        part, other = dot(near, weights[2][:, cols]), dot(far, weights[5][:, cols])
        here = refs[6][:, cols] if begun else part[:half]
        own_ref[:, cols] = here + other[:half]
        sent_ref[:, cols] = (part[-half:] + other[half:]).astype(jnp.bfloat16)


def mix_kernel(experts, capacity, hidden_ref, slot_ref, weight_ref, own_ref, other_ref, *refs):
    rows_refs, out_ref = refs[:-1], refs[-1]
    tokens, width = hidden_ref.shape
    line = lax.broadcasted_iota(jnp.int32, (tokens, capacity), 1).astype(jnp.float32)
    placed = [(line == slot_ref[:, d : d + 1]).astype(jnp.bfloat16) for d in range(experts)]
    step = columns_of(width)
    for c in range(0, width, step):
        cols = slice(c, c + step)
        total = hidden_ref[:, cols].astype(jnp.float32)
        for d in range(experts):
            if d:
                rows = rows_refs[d - 1][:, cols]
            else:
                rows = (own_ref[:, cols] + other_ref[:, cols].astype(jnp.float32)).astype(jnp.bfloat16)
            total += weight_ref[:, d : d + 1] * dot(placed[d], rows)
        out_ref[:, cols] = total.astype(jnp.bfloat16)


def body(hidden, lengths, norm_gain, w_gate, w_up, w_down, expert_ids, gate_weights):
    tokens_here, width = hidden.shape
    topk = expert_ids.shape[1]
    ranks = lax.axis_size("ep")
    experts = ranks // SPLIT
    capacity = SPLIT * ((3 * tokens_here * topk + 2 * experts * SPLIT - 1) // (2 * experts * SPLIT))
    capacity = -(-capacity // 16) * 16
    ff = w_gate.shape[-1]
    plane = (lax.axis_index("ep") // SPLIT).astype(jnp.int32).reshape(1)

    swap_core = [(i, i ^ 1) for i in range(ranks)]
    swap_side = [(i, i ^ 2) for i in range(ranks)]

    def shift(d):
        return [(i, (i + SPLIT * d) % ranks) for i in range(ranks)]

    def struct(rows, cols, dtype):
        return jax.ShapeDtypeStruct((rows, cols), dtype)

    lines = max(8, -(-experts // 8) * 8)
    block = struct(capacity, width, jnp.bfloat16)
    *packed, slot, weight = pl.pallas_call(
        functools.partial(pack_kernel, experts, capacity),
        out_shape=[block] * experts + [struct(tokens_here, lines, jnp.float32)] * 2,
        in_specs=[SMEM, SMEM, VMEM, VMEM, VMEM, VMEM],
        out_specs=[VMEM] * (experts + 2),
        compiler_params=pltpu.CompilerParams(vmem_limit_bytes=VMEM_BYTES),
    )(plane, lengths, hidden, norm_gain, expert_ids.T, gate_weights.T)

    def after(value, *others):
        return lax.optimization_barrier((value, *others))[0]

    params = dict(
        compiler_params=pltpu.CompilerParams(vmem_limit_bytes=32 << 20),
        cost_estimate=pl.CostEstimate(flops=1, bytes_accessed=1, transcendentals=0),
    )

    def expert(*operands):
        return pl.pallas_call(
            functools.partial(expert_kernel, len(operands) > 8),
            out_shape=[struct(capacity, width, jnp.float32), block],
            in_specs=[VMEM] * len(operands),
            out_specs=[VMEM, VMEM],
            **params,
        )(*operands)

    def first(*operands):
        return pl.pallas_call(
            first_kernel,
            out_shape=struct(capacity, width, jnp.float32),
            in_specs=[VMEM] * 4,
            out_specs=VMEM,
            **params,
        )(*operands)

    def across(rows):
        return lax.ppermute(rows, "ep", swap_side)

    order = [2, 1, 3] if experts == 4 else list(range(1, experts))
    count = len(order)
    theirs = across(packed[0])
    arrived = [lax.ppermute(packed[order[0]], "ep", shift(order[0]))]
    own_weights = (w_gate[0], w_up[0], w_down[0])
    weights = own_weights + tuple(lax.ppermute(after(w, packed[0]), "ep", swap_core) for w in own_weights)

    def send_along(i, *tied):
        arrived.append(lax.ppermute(after(packed[order[i]], *tied), "ep", shift(order[i])))

    own_here, sent_here = expert(packed[0], theirs, *weights, first(packed[0], *own_weights))
    other_here = across(sent_here)
    crossed = [across(after(arrived[0], other_here))]
    if count > 1:
        send_along(1, arrived[0], other_here)
    own, sent, other, rows, back = [], [], [], [], {}

    def send_back(i, *tied):
        rows.append((own[i] + after(other[i], *tied).astype(jnp.float32)).astype(jnp.bfloat16))
        back[order[i]] = lax.ppermute(rows[i], "ep", shift(experts - order[i]))

    for i in range(count):
        tied = [] if i else [other_here]
        if i > 1:
            tied.append(rows[i - 2])
        if i + 1 < count:
            crossed.append(across(after(arrived[i + 1], sent[i - 1] if i else other_here)))
            tied.append(arrived[i + 1])
        if i + 2 < count:
            send_along(i + 2, arrived[i + 1])
        mine_sum, their_part = expert(arrived[i], after(crossed[i], *tied), *weights)
        own.append(mine_sum)
        sent.append(their_part)
        if i:
            send_back(i - 1, sent[i])
        other.append(across(after(sent[i], rows[i - 1]) if i > 1 else sent[i]))
    send_back(count - 1, *(back[d] for d in order[:-2]))
    back[0] = (own_here, other_here)
    return pl.pallas_call(
        functools.partial(mix_kernel, experts, capacity),
        out_shape=struct(tokens_here, width, jnp.bfloat16),
        in_specs=[VMEM] * (experts + 4),
        out_specs=VMEM,
        compiler_params=pltpu.CompilerParams(vmem_limit_bytes=16 << 20),
    )(hidden, slot, weight, *back[0], *(back[d] for d in range(1, experts)))


def solution(mesh):
    return jax.shard_map(
        body,
        mesh=mesh,
        in_specs=(
            P(("group", "ep"), None),
            P(("group", "ep")),
            P(),
            P("ep", None, None),
            P("ep", None, None),
            P("ep", None, None),
            P(("group", "ep"), None),
            P(("group", "ep"), None),
        ),
        out_specs=P(("group", "ep"), None),
        check_vma=False,
    )
```
